128 devices in a mesh: layer: 4 (over z), leaf: 32 (over x, y, core).
Axes of the slice: x: 4, y: 4, z: 4, core: 2. Of those that a mesh axis runs over, the one named last changes fastest.
Arguments:
- sources: float32 [2, 4, 32, 384, 256], P(None, 'layer', 'leaf'), may hold values from -6 to 6
- leaf_inverse: float32 [2, 4, 32, 384, 384], P(None, 'layer', 'leaf'), may hold values from -0.21875 to 0.21875
- tree_up: float32 [2, 4, 32, 5, 384, 384], P(None, 'layer', 'leaf'), may hold values from -0.0546875 to 0.0546875
- tree_down: float32 [2, 4, 32, 5, 384, 384], P(None, 'layer', 'leaf'), may hold values from -0.0546875 to 0.0546875
- coupling: float32 [2, 4, 32, 384, 128], P(None, 'layer', 'leaf'), may hold values from -0.1875 to 0.1875
- index_map: int32 [4, 32, 384], P('layer', 'leaf'), may hold values from 0 to 383, each once within a row
Outputs:
- solution: float32 [2, 4, 32, 384, 256], P(None, 'layer', 'leaf')
The draws below stay inside these ranges and needn't reach their ends.
Inputs may be any that keep to these rules, and one draw needn't show every extreme that they name: `index_map`: each row of the last dimension holds every number from 0 to 383 once.
All inputs are finite; a program needn't handle non-finite values.
Results may differ from the reference program's by a relative error of at most 0.0001.
Values sent between devices are 32-bit elements; how exact they have to be, the bound alone decides.
A program may use at most 128 MiB of HBM per device.

```python
import jax
import jax.numpy as jnp
from jax import lax

R = 384
BND = 128
RHS = 256
LAYERS = 4
LEAVES = 32
LEVELS = 5


def steps_of(key, extent, shards, least, top_value):
    gain, own = 1.0, jax.random.fold_in(key, 6)
    for axis_at, shards_of in shards:
        steps = jnp.exp(jax.random.uniform(jax.random.fold_in(own, axis_at), (shards_of,), jnp.float32, least / len(shards), top_value / len(shards)))
        gain = gain * jnp.repeat(steps, extent[axis_at] // shards_of).reshape([-1 if axis == axis_at else 1 for axis in range(len(extent))])
    return gain


def normal_values(stream_key, extent, width, reach, shards=(), dtype=jnp.bfloat16):
    gain = steps_of(stream_key, extent, shards, -0.22, 0.18) if shards else 1.0
    result = jax.random.normal(stream_key, extent, jnp.float32) * width * gain
    return jnp.minimum(jnp.maximum(result, -reach), reach).astype(dtype)


def setup_inputs(seed: int = 0) -> dict:
    key_list = jax.random.split(jax.random.key(seed), 7)
    return {
        "sources": normal_values(key_list[0], (2, LAYERS, LEAVES, R, RHS), 1.0, 6.0, ((1, 4), (2, 32)), jnp.float32),
        "leaf_inverse": normal_values(key_list[1], (2, LAYERS, LEAVES, R, R), (2 * R) ** -0.5, 0.21875, ((1, 4), (2, 32)), jnp.float32),
        "tree_up": normal_values(key_list[2], (2, LAYERS, LEAVES, LEVELS, R, R), (32 * R) ** -0.5, 0.0546875, ((1, 4), (2, 32)), jnp.float32),
        "tree_down": normal_values(key_list[3], (2, LAYERS, LEAVES, LEVELS, R, R), (32 * R) ** -0.5, 0.0546875, ((1, 4), (2, 32)), jnp.float32),
        "coupling": normal_values(key_list[4], (2, LAYERS, LEAVES, R, BND), (8 * BND) ** -0.5, 0.1875, ((1, 4), (2, 32)), jnp.float32),
        "index_map": jax.vmap(lambda own: jax.random.permutation(own, R))(jax.random.split(key_list[5], LAYERS * LEAVES)).reshape((LAYERS, LEAVES, R)).astype(jnp.int32),
    }


def complex_apply(matrix, vector):
    highest = lax.Precision.HIGHEST
    real_real = jnp.matmul(matrix[0], vector[0], precision=highest)
    imag_imag = jnp.matmul(matrix[1], vector[1], precision=highest)
    real_imag = jnp.matmul(matrix[0], vector[1], precision=highest)
    imag_real = jnp.matmul(matrix[1], vector[0], precision=highest)
    return jnp.stack([real_real - imag_imag, real_imag + imag_real])


def partner(frontal, tree_bit):
    spread = 2 ** tree_bit
    shaped = frontal.reshape(2, LEAVES // (2 * spread), 2, spread, R, RHS)
    return shaped[:, :, ::-1].reshape(frontal.shape)


def reference(sources, leaf_inverse, tree_up, tree_down, coupling, index_map):
    leaf_ids = jnp.arange(LEAVES).astype(jnp.int32)[:, None]
    front_undo = jnp.argsort(index_map, axis=-1).astype(jnp.int32)
    previous = jnp.zeros((2, LEAVES, BND, RHS), jnp.float32)
    solved_layers = []
    for layer_index in range(LAYERS):
        reduced = sources[:, layer_index] - complex_apply(coupling[:, layer_index], previous)
        frontal = reduced[:, leaf_ids, index_map[layer_index], :]
        frontal = complex_apply(leaf_inverse[:, layer_index], frontal)
        for tree_bit in range(LEVELS):
            frontal = frontal + complex_apply(tree_up[:, layer_index, :, tree_bit], partner(frontal, tree_bit))
        for tree_bit in reversed(range(LEVELS)):
            frontal = frontal + complex_apply(tree_down[:, layer_index, :, tree_bit], partner(frontal, tree_bit))
        solved = frontal[:, leaf_ids, front_undo[layer_index], :]
        solved_layers.append(solved)
        previous = solved[:, :, R - BND:, :]
    return jnp.stack(solved_layers, axis=1)
```

```python
import jax
import jax.numpy as jnp
from jax import lax
from jax.experimental import pallas as pl
from jax.experimental.pallas import tpu as pltpu
from jax.sharding import PartitionSpec as P

MESH = pl.DeviceIdType.MESH
F32, BF16 = jnp.float32, jnp.bfloat16
WIDTH = 16
HOPS = (1, 2, 3, 4, 4, 3, 2, 1, 0)
LAST = len(HOPS) - 1


def split(x):
    high = x.astype(BF16)
    return high, (x - high.astype(F32)).astype(BF16)


def times(v, high, low):
    blocks, _, width, depth = v.shape
    rows, n = blocks * 2 * width, high.shape[1] // 2
    v_high, v_low = split(v.reshape(rows, depth))
    p = jnp.dot(jnp.concatenate([v_high, v_low], axis=0), high, preferred_element_type=F32)
    r = p[:rows] + p[rows:] + jnp.dot(v_high, low, preferred_element_type=F32)
    r = r.reshape(blocks, 2, width, 2 * n)
    return r[:, 0, :, :n] - r[:, 1, :, n:], r[:, 0, :, n:] + r[:, 1, :, :n]


def kernel(
    src_hbm, inv_hbm, up_hbm, down_hbm, cpl_hbm, row_ref, col_ref, out_ref,
    src, inv, up, down, cpl, wh, wl, ah, al, eh, el, place, pick, take,
    g, g_in, gt, gt_in, s, r, s_last, r_last, sb, rb,
    in_sem, g_send, g_recv, gt_send, gt_recv, send, recv, last_send, last_recv, b_send, b_recv,
):
    size = inv.shape[-1]
    border = cpl.shape[-1]
    columns = src.shape[-1]
    blocks = columns // WIDTH
    levels = up.shape[1]
    layers = lax.axis_size("layer")
    layer, leaf = lax.axis_index("layer"), lax.axis_index("leaf")

    def mirror(bit):
        spread = 1 << bit
        return leaf + (1 - 2 * ((leaf // spread) % 2)) * spread

    below, above = (layer + 1) % layers, (layer + layers - 1) % layers
    partners = [mirror(bit) for bit in range(levels)]

    loads = {}

    def load(name, source, target):
        loads[name] = pltpu.make_async_copy(source, target, in_sem.at[len(loads)])
        loads[name].start()

    load("inv", inv_hbm, inv)
    load("src", src_hbm, src)
    load("up0", up_hbm.at[:, 0], up.at[:, 0])
    load("cpl", cpl_hbm, cpl)
    for bit in range(1, levels):
        load(f"up{bit}", up_hbm.at[:, bit], up.at[:, bit])
    for bit in reversed(range(levels)):
        load(f"down{bit}", down_hbm.at[:, bit], down.at[:, bit])

    barrier = pltpu.get_barrier_semaphore()
    neighbours = [(layer, p) for p in partners]
    neighbours += [(z, q) for z in (below, above) for q in (leaf, partners[0])]
    for device in neighbours:
        pl.semaphore_signal(barrier, inc=1, device_id=device, device_id_type=MESH)

    lane = lax.broadcasted_iota(jnp.int32, (size, size), 1)
    sublane = lax.broadcasted_iota(jnp.int32, (size, size), 0)
    place[...] = jnp.where(sublane == row_ref[...], 1.0, 0.0).astype(BF16)
    pick[...] = jnp.where(lane == col_ref[...], 1.0, 0.0).astype(BF16)

    def prepare(at, matrix):
        for part in range(2):
            high, low = split(matrix[part].T)
            wh[at, :, part * size : (part + 1) * size] = high
            wl[at, :, part * size : (part + 1) * size] = low

    TOP, INV, DOWN0 = 8, 9, 10
    loads["inv"].wait()
    prepare(INV, inv)
    for w in (wh, wl):
        w[INV] = jnp.dot(place[...], w[INV], preferred_element_type=F32).astype(BF16)

    loads["src"].wait()
    for half in range(columns // 128):
        count = 128 // WIDTH
        for part in range(2):
            turned = src[part, :, half * 128 : (half + 1) * 128].T
            g[half * count : (half + 1) * count, part] = turned.reshape(count, WIDTH, size)
    pl.semaphore_wait(barrier, len(neighbours))

    CHUNK = 4
    chunks = blocks // CHUNK

    def g_copy(at):
        part = pl.ds(at * CHUNK, CHUNK)
        return pltpu.make_async_remote_copy(
            g.at[part], g_in.at[part], g_send.at[at], g_recv.at[at],
            device_id=(layer, partners[0]), device_id_type=MESH,
        )

    @pl.loop(0, chunks)
    def _(at):
        part = pl.ds(at * CHUNK, CHUNK)
        real, imag = times(g[part], wh[INV], wl[INV])
        g[part, 0] = real
        g[part, 1] = imag
        g_copy(at).start()

    loads["up0"].wait()
    prepare(TOP, up.at[:, 0])

    gt_copy = pltpu.make_async_remote_copy(
        gt, gt_in, gt_send, gt_recv, device_id=(layer, partners[0]), device_id_type=MESH
    )
    loads["cpl"].wait()

    @pl.when(layer > 0)
    def _():
        turned = jnp.stack([cpl[0].T, cpl[1].T])[None]
        real, imag = times(turned, wh[INV], wl[INV])
        gt[0, 0] = -real[0]
        gt[0, 1] = -imag[0]
        gt_copy.start()

    @pl.loop(0, chunks)
    def _(at):
        part = pl.ds(at * CHUNK, CHUNK)
        g_copy(at).wait()
        real, imag = times(g_in[part], wh[TOP], wl[TOP])
        g[part, 0] = g[part, 0] + real
        g[part, 1] = g[part, 1] + imag

    @pl.when(layer > 0)
    def _():
        gt_copy.wait()
        real, imag = times(gt_in[...], wh[TOP], wl[TOP])
        for row, pair in ((0, (gt[0, 0], gt[0, 1])), (border, (real[0], imag[0]))):
            for part in range(2):
                high, low = split(pair[part])
                ah[row : row + border, part * size : (part + 1) * size] = high
                al[row : row + border, part * size : (part + 1) * size] = low

    def b_copy(block, side):
        target = leaf if side == 0 else partners[0]
        return pltpu.make_async_remote_copy(
            sb.at[block], rb.at[block, side], b_send.at[block, side], b_recv.at[block, side],
            device_id=(below, target), device_id_type=MESH,
        )

    def f_copy(hop, block):
        slot = block % 2
        target = (layer, partners[HOPS[hop]])
        if hop == LAST:
            return pltpu.make_async_remote_copy(
                s_last.at[block], r_last.at[block], last_send.at[slot], last_recv.at[slot],
                device_id=target, device_id_type=MESH,
            )
        return pltpu.make_async_remote_copy(
            s.at[hop, slot], r.at[hop, slot], send.at[hop, slot], recv.at[hop, slot],
            device_id=target, device_id_type=MESH,
        )

    def front(hop, block):
        return s_last.at[block] if hop == LAST else s.at[hop, block % 2]

    def arrived(hop, block):
        return r_last.at[block] if hop == LAST else r.at[hop, block % 2]

    def stage_first(block):
        @pl.when(block >= 2)
        def _():
            f_copy(0, block - 2).wait_send()

        @pl.when(layer == 0)
        def _():
            front(0, block)[...] = g[block]

        @pl.when(layer > 0)
        def _():
            for side in range(2):
                b_copy(block, side).wait_recv()
            v = jnp.concatenate([rb[block, 0], rb[block, 1]], axis=-1)[None]
            real, imag = times(v, ah[...], al[...])
            front(0, block)[0] = g[block, 0] + real[0]
            front(0, block)[1] = g[block, 1] + imag[0]

        f_copy(0, block).start()

    def stage_middle(hop, block):
        @pl.when(block == 0)
        def _():
            name = f"up{hop}" if hop < levels else f"down{HOPS[hop - 1]}"
            loads[name].wait()
            level = HOPS[hop - 1]
            prepare(hop - 1, up.at[:, level] if hop < levels else down.at[:, level])

        @pl.when(block >= 2)
        def _():
            f_copy(hop, block - 2).wait_send()

        f_copy(hop - 1, block).wait_recv()
        real, imag = times(arrived(hop - 1, block)[...][None], wh[hop - 1], wl[hop - 1])
        front(hop, block)[0] = front(hop - 1, block)[0] + real[0]
        front(hop, block)[1] = front(hop - 1, block)[1] + imag[0]
        f_copy(hop, block).start()

    def stage_border(block):
        @pl.when(block == 0)
        def _():
            loads["down0"].wait()
            prepare(DOWN0, down.at[:, 0])
            take[...] = pick[:, size - border :]
            for w, e in ((wh, eh), (wl, el)):
                for part in range(2):
                    e[:, part * border : (part + 1) * border] = jnp.dot(
                        w[DOWN0, :, part * size : (part + 1) * size], take[...], preferred_element_type=F32
                    ).astype(BF16)

        @pl.when(layer < layers - 1)
        def _():
            high, low = split(front(LAST, block)[...].reshape(2 * WIDTH, size))
            own = jnp.dot(jnp.concatenate([high, low], axis=0), take[...], preferred_element_type=F32)
            own = (own[: 2 * WIDTH] + own[2 * WIDTH :]).reshape(2, WIDTH, border)
            f_copy(LAST, block).wait_recv()
            real, imag = times(arrived(LAST, block)[...][None], eh[...], el[...])
            sb[block, 0] = own[0] + real[0]
            sb[block, 1] = own[1] + imag[0]
            for side in range(2):
                b_copy(block, side).start()

        @pl.when(layer == layers - 1)
        def _():
            f_copy(LAST, block).wait_recv()

    def stage_output(half):
        count = 128 // WIDTH
        part = pl.ds(half * count, count)
        real, imag = times(r_last[part], wh[DOWN0], wl[DOWN0])
        for index, add in ((0, real), (1, imag)):
            x = (s_last[part, index] + add).reshape(128, size)
            y = None
            for term in split(x):
                product = jnp.dot(term, pick[...], preferred_element_type=F32)
                y = product if y is None else y + product
            out_ref[index, :, half * 128 : (half + 1) * 128] = y.T

    count = 128 // WIDTH

    @pl.loop(0, blocks + LAST + 1)
    def _(tick):
        for stage in reversed(range(LAST + 2)):
            block = tick - stage

            @pl.when(jnp.logical_and(block >= 0, block < blocks))
            def _():
                if stage == 0:
                    stage_first(block)
                elif stage <= LAST:
                    stage_middle(stage, block)
                else:
                    stage_border(block)

        for half in range(columns // 128):

            @pl.when(tick == LAST + 1 + (half + 1) * count - 1)
            def _():
                stage_output(half)

    for hop in range(LAST + 1):
        for block in (blocks - 2, blocks - 1):
            f_copy(hop, block).wait_send()

    @pl.when(layer < layers - 1)
    def _():
        @pl.loop(0, blocks)
        def _(block):
            for side in range(2):
                b_copy(block, side).wait_send()


def per_device(sources, leaf_inverse, tree_up, tree_down, coupling, index_map):
    size, columns = sources.shape[-2:]
    border = coupling.shape[-1]
    levels = tree_up.shape[3]
    blocks = columns // WIDTH
    operands = (
        sources.reshape(2, size, columns),
        leaf_inverse.reshape(2, size, size),
        tree_up.reshape(2, levels, size, size),
        tree_down.reshape(2, levels, size, size),
        coupling.reshape(2, size, border),
        index_map.reshape(1, size),
        index_map.reshape(size, 1),
    )
    vmem, dma = pltpu.VMEM, pltpu.SemaphoreType.DMA
    wide = 2 * size
    out = pl.pallas_call(
        kernel,
        out_shape=jax.ShapeDtypeStruct((2, size, columns), F32),
        in_specs=[pl.BlockSpec(memory_space=pl.ANY)] * 5 + [pl.BlockSpec(memory_space=pltpu.VMEM)] * 2,
        out_specs=pl.BlockSpec(memory_space=pltpu.VMEM),
        scratch_shapes=[
            vmem((2, size, columns), F32),
            vmem((2, size, size), F32),
            vmem((2, levels, size, size), F32),
            vmem((2, levels, size, size), F32),
            vmem((2, size, border), F32),
            vmem((11, size, wide), BF16),
            vmem((11, size, wide), BF16),
            vmem((2 * border, wide), BF16),
            vmem((2 * border, wide), BF16),
            vmem((size, 2 * border), BF16),
            vmem((size, 2 * border), BF16),
            vmem((size, size), BF16),
            vmem((size, size), BF16),
            vmem((size, border), BF16),
            vmem((blocks, 2, WIDTH, size), F32),
            vmem((blocks, 2, WIDTH, size), F32),
            vmem((1, 2, border, size), F32),
            vmem((1, 2, border, size), F32),
            vmem((LAST, 2, 2, WIDTH, size), F32),
            vmem((LAST, 2, 2, WIDTH, size), F32),
            vmem((blocks, 2, WIDTH, size), F32),
            vmem((blocks, 2, WIDTH, size), F32),
            vmem((blocks, 2, WIDTH, border), F32),
            vmem((blocks, 2, 2, WIDTH, border), F32),
            dma((3 + 2 * levels,)),
            dma((blocks // 4,)),
            dma((blocks // 4,)),
            dma,
            dma,
            dma((LAST, 2)),
            dma((LAST, 2)),
            dma((2,)),
            dma((2,)),
            dma((blocks, 2)),
            dma((blocks, 2)),
        ],
        compiler_params=pltpu.CompilerParams(
            collective_id=0, has_side_effects=True, vmem_limit_bytes=56 * 1024 * 1024
        ),
        name="sweep",
    )(*operands)
    return out.reshape(sources.shape)


def solution(mesh):
    placed = (
        P(None, "layer", "leaf", None, None),
        P(None, "layer", "leaf", None, None),
        P(None, "layer", "leaf", None, None, None),
        P(None, "layer", "leaf", None, None, None),
        P(None, "layer", "leaf", None, None),
        P("layer", "leaf", None),
    )
    return jax.shard_map(
        per_device,
        mesh=mesh,
        in_specs=placed,
        out_specs=P(None, "layer", "leaf", None, None),
        check_vma=False,
    )
```

```python
import jax
import jax.numpy as jnp
from jax import lax
from jax.experimental import pallas as pl
from jax.experimental.pallas import tpu as pltpu
from jax.sharding import PartitionSpec as P

MESH = pl.DeviceIdType.MESH
F32, BF16 = jnp.float32, jnp.bfloat16
WIDTH = 16
SLOTS = 4
CHUNK = 4

UP1, UP2, UP21, UP3, TURN, TURN2, DOWN3, DOWN1, DOWN2, DOWN12, UP0, INV, DOWN0 = range(13)
LAST = 9

PLAIN = (
    ((), None, False, ((0, 2),)),
    ((0,), UP1, False, ((1, 4),)),
    ((1,), UP2, False, ((3, 8),)),
    ((3,), UP3, False, ((4, 16),)),
    ((4,), TURN, False, ((2, 16),)),
    ((2,), TURN2, False, ((5, 8),)),
    ((5,), DOWN3, False, ((7, 4),)),
    ((7,), DOWN2, False, ((6, 2),)),
    ((6,), DOWN1, False, ((LAST, 1),)),
)
FUSED = (
    ((), None, False, ((1, 4), (0, 2), (2, 6))),
    ((0, 1, 2), UP1, False, ((3, 8),)),
    ((3,), UP3, False, ((4, 16),)),
    ((4,), TURN, True, ((5, 8),)),
    ((5,), DOWN3, False, ((7, 4), (6, 2), (8, 6))),
    ((6, 7, 8), DOWN1, False, ((LAST, 1),)),
)
MASKS = (1, 2, 4, 6, 8, 16)

PLAIN_ORDER = ((0, 0), (9, 12), (5, 8), (6, 9), (8, 11), (7, 10), (2, 3), (4, 6), (1, 1), (3, 4))
FUSED_ORDER = ((0, 0), (2, 3), (3, 4), (4, 5), (6, 7), (1, 1), (5, 6))


def split(x):
    high = x.astype(BF16)
    return high, (x - high.astype(F32)).astype(BF16)


def times(v, high, low):
    blocks, _, width, depth = v.shape
    rows, n = blocks * 2 * width, high.shape[1] // 2
    v_high, v_low = split(v.reshape(rows, depth))
    p = jnp.dot(jnp.concatenate([v_high, v_low], axis=0), high, preferred_element_type=F32)
    r = p[:rows] + p[rows:] + jnp.dot(v_high, low, preferred_element_type=F32)
    r = r.reshape(blocks, 2, width, 2 * n)
    return r[:, 0, :, :n] - r[:, 1, :, n:], r[:, 0, :, n:] + r[:, 1, :, :n]


def kernel(
    src_hbm, inv_hbm, up_hbm, down_hbm, cpl_hbm, row_ref, out_ref,
    src, inv, up, down, cpl, wh, wl, ah, al, eh, el, place, pick, take, far,
    g, g_in, gt, gt_in, s, r, s_last, r_last, sb, rb,
    in_sem, g_send, g_recv, gt_send, gt_recv, far_send, far_recv, send, recv, b_send, b_recv,
):
    size = inv.shape[-1]
    border = cpl.shape[-1]
    columns = src.shape[-1]
    blocks = columns // WIDTH
    levels = up.shape[1]
    layers = lax.axis_size("layer")
    layer, leaf = lax.axis_index("layer"), lax.axis_index("leaf")

    def mirror(mask):
        other = leaf
        for bit in range(levels):
            if mask >> bit & 1:
                other = other + (1 - 2 * ((leaf // (1 << bit)) % 2)) * (1 << bit)
        return other

    below, above = (layer + 1) % layers, (layer + layers - 1) % layers
    partners = {mask: mirror(mask) for mask in MASKS}

    loads = {}

    def load(name, source, target):
        loads[name] = pltpu.make_async_copy(source, target, in_sem.at[len(loads)])
        loads[name].start()

    load("inv", inv_hbm, inv)
    load("src", src_hbm, src)
    load("up0", up_hbm.at[:, 0], up.at[:, 0])

    barrier = pltpu.get_barrier_semaphore()
    neighbours = [(layer, p) for p in partners.values()]
    neighbours += [(z, q) for z in (below, above) for q in (leaf, partners[1])]
    for device in neighbours:
        pl.semaphore_signal(barrier, inc=1, device_id=device, device_id_type=MESH)

    sublane = lax.broadcasted_iota(jnp.int32, (size, size), 0)
    chosen = jnp.where(sublane == row_ref[...], 1.0, 0.0)
    place[...] = chosen.astype(BF16)
    pick[...] = chosen.T.astype(BF16)

    def prepare(at, *matrices):
        for part in range(2):
            total = matrices[0][part]
            for matrix in matrices[1:]:
                total = total + matrix[part]
            high, low = split(total.T)
            wh[at, :, part * size : (part + 1) * size] = high
            wl[at, :, part * size : (part + 1) * size] = low

    loads["inv"].wait()
    prepare(INV, inv)
    for w in (wh, wl):
        w[INV] = jnp.dot(place[...], w[INV], preferred_element_type=F32).astype(BF16)

    loads["src"].wait()
    for bit in (1, 4):
        load(f"up{bit}", up_hbm.at[:, bit], up.at[:, bit])
    load("cpl", cpl_hbm, cpl)
    load("down2", down_hbm.at[:, 2], down.at[:, 2])
    for bit in (2, 3):
        load(f"up{bit}", up_hbm.at[:, bit], up.at[:, bit])
    for bit in (4, 3, 1, 0):
        load(f"down{bit}", down_hbm.at[:, bit], down.at[:, bit])

    for half in range(columns // 128):
        count = 128 // WIDTH
        for part in range(2):
            turned = src[part, :, half * 128 : (half + 1) * 128].T
            g[half * count : (half + 1) * count, part] = turned.reshape(count, WIDTH, size)
    pl.semaphore_wait(barrier, len(neighbours))

    chunks = blocks // CHUNK

    def g_copy(at):
        part = pl.ds(at * CHUNK, CHUNK)
        return pltpu.make_async_remote_copy(
            g.at[part], g_in.at[part], g_send.at[at], g_recv.at[at],
            device_id=(layer, partners[1]), device_id_type=MESH,
        )

    def far_copy(at, source, mask):
        return pltpu.make_async_remote_copy(
            source, far.at[at], far_send.at[at], far_recv.at[at],
            device_id=(layer, partners[mask]), device_id_type=MESH,
        )

    up1_copy = far_copy(0, up.at[:, 1], 4)
    up4_copy = far_copy(1, up.at[:, 4], 16)
    down2_copy = far_copy(2, down.at[:, 2], 2)

    @pl.when(layer > 0)
    def _():
        loads["up1"].wait()
        up1_copy.start()
        loads["up4"].wait()
        up4_copy.start()

    @pl.loop(0, chunks)
    def _(at):
        part = pl.ds(at * CHUNK, CHUNK)
        real, imag = times(g[part], wh[INV], wl[INV])
        g[part, 0] = real
        g[part, 1] = imag
        g_copy(at).start()

    loads["up0"].wait()
    prepare(UP0, up.at[:, 0])

    def couple(at):
        part = pl.ds(at * CHUNK, CHUNK)
        g_copy(at).wait()
        real, imag = times(g_in[part], wh[UP0], wl[UP0])
        g[part, 0] = g[part, 0] + real
        g[part, 1] = g[part, 1] + imag

    def product(at, by, matrix):
        for low_row in range(0, size, 128):
            rows = slice(low_row, low_row + 128)
            v = jnp.stack([matrix[0, :, rows].T, matrix[1, :, rows].T])[None]
            for part, value in enumerate(times(v, wh[by], wl[by])):
                high, low = split(value[0])
                wh[at, rows, part * size : (part + 1) * size] = high
                wl[at, rows, part * size : (part + 1) * size] = low

    def prepare_border():
        loads["down0"].wait()
        prepare(DOWN0, down.at[:, 0])
        take[...] = pick[:, size - border :]
        for w, e in ((wh, eh), (wl, el)):
            for part in range(2):
                e[:, part * border : (part + 1) * border] = jnp.dot(
                    w[DOWN0, :, part * size : (part + 1) * size], take[...], preferred_element_type=F32
                ).astype(BF16)

    gt_copy = pltpu.make_async_remote_copy(
        gt, gt_in, gt_send, gt_recv, device_id=(layer, partners[1]), device_id_type=MESH
    )
    sources_of = {
        UP1: ("up1", up.at[:, 1]), UP2: ("up2", up.at[:, 2]), UP3: ("up3", up.at[:, 3]), TURN: ("up4", up.at[:, 4]),
        TURN2: ("down4", down.at[:, 4]), DOWN3: ("down3", down.at[:, 3]), DOWN1: ("down1", down.at[:, 1]),
        DOWN2: ("down2", down.at[:, 2]),
    }

    @pl.when(layer > 0)
    def _():
        loads["cpl"].wait()
        turned = jnp.stack([cpl[0].T, cpl[1].T])[None]
        real, imag = times(turned, wh[INV], wl[INV])
        gt[0, 0] = -real[0]
        gt[0, 1] = -imag[0]
        gt_copy.start()

        @pl.loop(0, chunks)
        def _(at):
            couple(at)

        gt_copy.wait()
        real, imag = times(gt_in[...], wh[UP0], wl[UP0])
        for row, pair in ((0, (gt[0, 0], gt[0, 1])), (border, (real[0], imag[0]))):
            for part in range(2):
                high, low = split(pair[part])
                ah[row : row + border, part * size : (part + 1) * size] = high
                al[row : row + border, part * size : (part + 1) * size] = low

        for at, (name, matrix) in sources_of.items():
            if at != TURN:
                if at != UP1:
                    loads[name].wait()
                prepare(at, matrix)
        prepare_border()
        up1_copy.wait()
        down2_copy.start()
        product(UP21, UP2, far.at[0])
        up4_copy.wait()
        product(TURN, TURN2, far.at[1])
        prepare(TURN2, up.at[:, 4], down.at[:, 4])
        down2_copy.wait()
        product(DOWN12, DOWN1, far.at[2])

    @pl.when(layer == 0)
    def _():
        loads["cpl"].wait()

    def b_copy(block, side):
        target = partners[1] if side else leaf
        return pltpu.make_async_remote_copy(
            sb.at[block], rb.at[block, side], b_send.at[side], b_recv.at[block, side],
            device_id=(below, target), device_id_type=MESH,
        )

    def sweep(moves, order, plain):
        lags = dict(order)
        final = len(moves)

        def front(stage, block):
            return s_last.at[block] if stage == final - 1 else s.at[stage, block]

        def arrived(lane, block):
            return r_last.at[block] if lane == LAST else r.at[lane, block % SLOTS]

        def f_copy(stage, lane, mask, block):
            return pltpu.make_async_remote_copy(
                front(stage, block), arrived(lane, block), send.at[lane], recv.at[lane, block % SLOTS],
                device_id=(layer, partners[mask]), device_id_type=MESH,
            )

        senders = {lane: (stage, mask) for stage, move in enumerate(moves) for lane, mask in move[3]}

        def receive(lane, block):
            stage, mask = senders[lane]
            f_copy(stage, lane, mask, block).wait_recv()

        def stage_first(block):
            if plain:

                @pl.when(block % CHUNK == 0)
                def _():
                    couple(block // CHUNK)

                front(0, block)[...] = g[block]
            else:
                for side in range(2):
                    b_copy(block, side).wait_recv()
                v = jnp.concatenate([rb[block, 0], rb[block, 1]], axis=-1)[None]
                real, imag = times(v, ah[...], al[...])
                front(0, block)[0] = g[block, 0] + real[0]
                front(0, block)[1] = g[block, 1] + imag[0]

        def stage_middle(stage, block):
            lanes, at, own, _ = moves[stage]
            if plain:

                @pl.when(block == 0)
                def _():
                    name, matrix = sources_of[at]
                    loads[name].wait()
                    prepare(at, matrix)

            for lane in lanes:
                receive(lane, block)
            terms = [front(stage - 1, block)[...]] if own else []
            terms += [arrived(lane, block)[...] for lane in lanes]
            count = len(terms)
            v = terms[0] if count == 1 else jnp.concatenate(terms, axis=-1)
            high = wh[at : at + count].reshape(count * size, 2 * size)
            low = wl[at : at + count].reshape(count * size, 2 * size)
            real, imag = times(v[None], high, low)
            front(stage, block)[0] = front(stage - 1, block)[0] + real[0]
            front(stage, block)[1] = front(stage - 1, block)[1] + imag[0]

        def stage_border(block):
            if plain:

                @pl.when(block == 0)
                def _():
                    prepare_border()

            @pl.when(layer < layers - 1)
            def _():
                high, low = split(front(final - 1, block)[...].reshape(2 * WIDTH, size))
                own = jnp.dot(jnp.concatenate([high, low], axis=0), take[...], preferred_element_type=F32)
                own = (own[: 2 * WIDTH] + own[2 * WIDTH :]).reshape(2, WIDTH, border)
                receive(LAST, block)
                real, imag = times(arrived(LAST, block)[...][None], eh[...], el[...])
                sb[block, 0] = own[0] + real[0]
                sb[block, 1] = own[1] + imag[0]
                for side in range(2):
                    b_copy(block, side).start()

            @pl.when(layer == layers - 1)
            def _():
                receive(LAST, block)

        count = 128 // WIDTH

        def stage_output(half):
            part = pl.ds(half * count, count)
            real, imag = times(r_last[part], wh[DOWN0], wl[DOWN0])
            for index, add in ((0, real), (1, imag)):
                x = (s_last[part, index] + add).reshape(128, size)
                y = None
                for term in split(x):
                    value = jnp.dot(term, pick[...], preferred_element_type=F32)
                    y = value if y is None else y + value
                out_ref[index, :, half * 128 : (half + 1) * 128] = y.T

        @pl.loop(0, blocks + max(lags.values()))
        def _(tick):
            for stage, lag in order:
                block = tick - lag

                @pl.when(jnp.logical_and(block >= 0, block < blocks))
                def _():
                    if stage == final:
                        stage_border(block)
                        return
                    if stage == 0:
                        stage_first(block)
                    else:
                        stage_middle(stage, block)
                    for lane, mask in moves[stage][3]:
                        f_copy(stage, lane, mask, block).start()

            for half in range(columns // 128):

                @pl.when(tick == lags[final] + (half + 1) * count - 1)
                def _():
                    stage_output(half)

        for lane, (stage, mask) in senders.items():
            every = s_last if lane == LAST else s.at[stage]
            pltpu.make_async_remote_copy(
                every, every, send.at[lane], recv.at[0, 0], device_id=(layer, partners[mask]), device_id_type=MESH
            ).wait_send()

    @pl.when(layer == 0)
    def _():
        sweep(PLAIN, PLAIN_ORDER, True)

    @pl.when(layer > 0)
    def _():
        sweep(FUSED, FUSED_ORDER, False)

    @pl.when(layer < layers - 1)
    def _():
        for side in range(2):
            pltpu.make_async_remote_copy(
                sb, sb, b_send.at[side], b_recv.at[0, 0], device_id=(below, leaf), device_id_type=MESH
            ).wait_send()


def per_device(sources, leaf_inverse, tree_up, tree_down, coupling, index_map):
    size, columns = sources.shape[-2:]
    border = coupling.shape[-1]
    levels = tree_up.shape[3]
    blocks = columns // WIDTH
    operands = (
        sources.reshape(2, size, columns),
        leaf_inverse.reshape(2, size, size),
        tree_up.reshape(2, levels, size, size),
        tree_down.reshape(2, levels, size, size),
        coupling.reshape(2, size, border),
        index_map.reshape(1, size),
    )
    vmem, dma = pltpu.VMEM, pltpu.SemaphoreType.DMA
    wide = 2 * size
    out = pl.pallas_call(
        kernel,
        out_shape=jax.ShapeDtypeStruct((2, size, columns), F32),
        in_specs=[pl.BlockSpec(memory_space=pl.ANY)] * 5 + [pl.BlockSpec(memory_space=pltpu.VMEM)],
        out_specs=pl.BlockSpec(memory_space=pltpu.VMEM),
        scratch_shapes=[
            vmem((2, size, columns), F32),
            vmem((2, size, size), F32),
            vmem((2, levels, size, size), F32),
            vmem((2, levels, size, size), F32),
            vmem((2, size, border), F32),
            vmem((13, size, wide), BF16),
            vmem((13, size, wide), BF16),
            vmem((2 * border, wide), BF16),
            vmem((2 * border, wide), BF16),
            vmem((size, 2 * border), BF16),
            vmem((size, 2 * border), BF16),
            vmem((size, size), BF16),
            vmem((size, size), BF16),
            vmem((size, border), BF16),
            vmem((3, 2, size, size), F32),
            vmem((blocks, 2, WIDTH, size), F32),
            vmem((blocks, 2, WIDTH, size), F32),
            vmem((1, 2, border, size), F32),
            vmem((1, 2, border, size), F32),
            vmem((len(PLAIN) - 1, blocks, 2, WIDTH, size), F32),
            vmem((LAST, SLOTS, 2, WIDTH, size), F32),
            vmem((blocks, 2, WIDTH, size), F32),
            vmem((blocks, 2, WIDTH, size), F32),
            vmem((blocks, 2, WIDTH, border), F32),
            vmem((blocks, 2, 2, WIDTH, border), F32),
            dma((4 + 2 * levels,)),
            dma((blocks // CHUNK,)),
            dma((blocks // CHUNK,)),
            dma,
            dma,
            dma((3,)),
            dma((3,)),
            dma((LAST + 1,)),
            dma((LAST + 1, SLOTS)),
            dma((2,)),
            dma((blocks, 2)),
        ],
        compiler_params=pltpu.CompilerParams(
            collective_id=0, has_side_effects=True, vmem_limit_bytes=60 * 1024 * 1024
        ),
        name="sweep",
    )(*operands)
    return out.reshape(sources.shape)


def solution(mesh):
    placed = (
        P(None, "layer", "leaf", None, None),
        P(None, "layer", "leaf", None, None),
        P(None, "layer", "leaf", None, None, None),
        P(None, "layer", "leaf", None, None, None),
        P(None, "layer", "leaf", None, None),
        P("layer", "leaf", None),
    )
    return jax.shard_map(
        per_device,
        mesh=mesh,
        in_specs=placed,
        out_specs=P(None, "layer", "leaf", None, None),
        check_vma=False,
    )
```

```python
import jax
import jax.numpy as jnp
from jax import lax
from jax.experimental import pallas as pl
from jax.experimental.pallas import tpu as pltpu
from jax.sharding import PartitionSpec as P

MESH = pl.DeviceIdType.MESH
F32, BF16 = jnp.float32, jnp.bfloat16
WIDTH = 16
SLOTS = 4
CHUNK = 4

UP1, UP2, UP21, UP3, TURN, TURN2, DOWN3, DOWN1, DOWN2, DOWN12, UP0, INV, DOWN0 = range(13)
LAST = 9

PLAIN = (
    ((), None, False, ((0, 2),)),
    ((0,), UP1, False, ((1, 4),)),
    ((1,), UP2, False, ((3, 8),)),
    ((3,), UP3, False, ((4, 16),)),
    ((4,), TURN, False, ((2, 16),)),
    ((2,), TURN2, False, ((5, 8),)),
    ((5,), DOWN3, False, ((7, 4),)),
    ((7,), DOWN2, False, ((6, 2),)),
    ((6,), DOWN1, False, ((LAST, 1),)),
)
FUSED = (
    ((), None, False, ((1, 4), (0, 2), (2, 6))),
    ((0, 1, 2), UP1, False, ((3, 8),)),
    ((3,), UP3, False, ((4, 16),)),
    ((4,), TURN, True, ((5, 8),)),
    ((5,), DOWN3, False, ((7, 4), (6, 2), (8, 6))),
    ((6, 7, 8), DOWN1, False, ((LAST, 1),)),
)
MASKS = (1, 2, 4, 6, 8, 16)
LATE = 3

PLAIN_ORDER = ((0, 0), (9, 12), (5, 8), (6, 9), (8, 11), (7, 10), (2, 3), (4, 6), (1, 1), (3, 4))
FUSED_ORDER = ((0, 0), (2, 3), (3, 4), (4, 5), (6, 7), (1, 1), (5, 6))


def split(x):
    high = x.astype(BF16)
    return high, (x - high.astype(F32)).astype(BF16)


def times(v, high, low):
    blocks, _, width, depth = v.shape
    rows, n = blocks * 2 * width, high.shape[1] // 2
    v_high, v_low = split(v.reshape(rows, depth))
    p = jnp.dot(jnp.concatenate([v_high, v_low], axis=0), high, preferred_element_type=F32)
    r = p[:rows] + p[rows:] + jnp.dot(v_high, low, preferred_element_type=F32)
    r = r.reshape(blocks, 2, width, 2 * n)
    return r[:, 0, :, :n] - r[:, 1, :, n:], r[:, 0, :, n:] + r[:, 1, :, :n]


def kernel(
    src_hbm, inv_hbm, up_hbm, down_hbm, cpl_hbm, row_ref, out_ref,
    src, inv, up, down, cpl, wh, wl, ah, al, eh, el, place, pick, take, far,
    g, g_in, gt, gt_in, s, r, s_last, r_last, sb, rb,
    in_sem, g_send, g_recv, gt_send, gt_recv, far_send, far_recv, send, recv, b_send, b_recv,
):
    size = inv.shape[-1]
    border = cpl.shape[-1]
    columns = src.shape[-1]
    blocks = columns // WIDTH
    levels = up.shape[1]
    layers = lax.axis_size("layer")
    layer, leaf = lax.axis_index("layer"), lax.axis_index("leaf")

    def mirror(mask):
        other = leaf
        for bit in range(levels):
            if mask >> bit & 1:
                other = other + (1 - 2 * ((leaf // (1 << bit)) % 2)) * (1 << bit)
        return other

    below, above = (layer + 1) % layers, (layer + layers - 1) % layers
    partners = {mask: mirror(mask) for mask in MASKS}

    loads = {}

    def load(name, source, target):
        loads[name] = pltpu.make_async_copy(source, target, in_sem.at[len(loads)])
        loads[name].start()

    load("inv", inv_hbm, inv)
    load("src", src_hbm, src)
    load("up0", up_hbm.at[:, 0], up.at[:, 0])

    barrier = pltpu.get_barrier_semaphore()
    neighbours = [(layer, p) for p in partners.values()]
    neighbours += [(z, q) for z in (below, above) for q in (leaf, partners[1])]
    for device in neighbours:
        pl.semaphore_signal(barrier, inc=1, device_id=device, device_id_type=MESH)

    sublane = lax.broadcasted_iota(jnp.int32, (size, size), 0)
    chosen = jnp.where(sublane == row_ref[...], 1.0, 0.0)
    place[...] = chosen.astype(BF16)
    pick[...] = chosen.T.astype(BF16)

    def prepare(at, *matrices):
        for part in range(2):
            total = matrices[0][part]
            for matrix in matrices[1:]:
                total = total + matrix[part]
            high, low = split(total.T)
            wh[at, :, part * size : (part + 1) * size] = high
            wl[at, :, part * size : (part + 1) * size] = low

    loads["inv"].wait()
    prepare(INV, inv)
    for w in (wh, wl):
        w[INV] = jnp.dot(place[...], w[INV], preferred_element_type=F32).astype(BF16)

    loads["src"].wait()
    for bit in (1, 4):
        load(f"up{bit}", up_hbm.at[:, bit], up.at[:, bit])
    load("cpl", cpl_hbm, cpl)
    load("down2", down_hbm.at[:, 2], down.at[:, 2])
    for bit in (2, 3):
        load(f"up{bit}", up_hbm.at[:, bit], up.at[:, bit])
    for bit in (4, 3, 1, 0):
        load(f"down{bit}", down_hbm.at[:, bit], down.at[:, bit])

    for half in range(columns // 128):
        count = 128 // WIDTH
        for part in range(2):
            turned = src[part, :, half * 128 : (half + 1) * 128].T
            g[half * count : (half + 1) * count, part] = turned.reshape(count, WIDTH, size)
    pl.semaphore_wait(barrier, len(neighbours))

    chunks = blocks // CHUNK

    def g_copy(at):
        part = pl.ds(at * CHUNK, CHUNK)
        return pltpu.make_async_remote_copy(
            g.at[part], g_in.at[part], g_send.at[at], g_recv.at[at],
            device_id=(layer, partners[1]), device_id_type=MESH,
        )

    def far_copy(at, source, mask):
        return pltpu.make_async_remote_copy(
            source, far.at[at], far_send.at[at], far_recv.at[at],
            device_id=(layer, partners[mask]), device_id_type=MESH,
        )

    up1_copy = far_copy(0, up.at[:, 1], 4)
    up4_copy = far_copy(1, up.at[:, 4], 16)
    down2_copy = far_copy(2, down.at[:, 2], 2)

    @pl.when(layer > 0)
    def _():
        loads["up1"].wait()
        up1_copy.start()
        loads["up4"].wait()
        up4_copy.start()

    @pl.loop(0, chunks)
    def _(at):
        part = pl.ds(at * CHUNK, CHUNK)
        real, imag = times(g[part], wh[INV], wl[INV])
        g[part, 0] = real
        g[part, 1] = imag
        g_copy(at).start()

    loads["up0"].wait()
    prepare(UP0, up.at[:, 0])

    def couple(at):
        part = pl.ds(at * CHUNK, CHUNK)
        g_copy(at).wait()
        real, imag = times(g_in[part], wh[UP0], wl[UP0])
        g[part, 0] = g[part, 0] + real
        g[part, 1] = g[part, 1] + imag

    def product(at, by, matrix, parts=(0, 1, 2)):
        for low_row in (part * (size // 3) for part in parts):
            rows = slice(low_row, low_row + 128)
            v = jnp.stack([matrix[0, :, rows].T, matrix[1, :, rows].T])[None]
            for part, value in enumerate(times(v, wh[by], wl[by])):
                high, low = split(value[0])
                wh[at, rows, part * size : (part + 1) * size] = high
                wl[at, rows, part * size : (part + 1) * size] = low

    def prepare_border():
        loads["down0"].wait()
        prepare(DOWN0, down.at[:, 0])
        take[...] = pick[:, size - border :]
        for w, e in ((wh, eh), (wl, el)):
            for part in range(2):
                e[:, part * border : (part + 1) * border] = jnp.dot(
                    w[DOWN0, :, part * size : (part + 1) * size], take[...], preferred_element_type=F32
                ).astype(BF16)

    gt_copy = pltpu.make_async_remote_copy(
        gt, gt_in, gt_send, gt_recv, device_id=(layer, partners[1]), device_id_type=MESH
    )
    sources_of = {
        UP1: ("up1", up.at[:, 1]), UP2: ("up2", up.at[:, 2]), UP3: ("up3", up.at[:, 3]), TURN: ("up4", up.at[:, 4]),
        TURN2: ("down4", down.at[:, 4]), DOWN3: ("down3", down.at[:, 3]), DOWN1: ("down1", down.at[:, 1]),
        DOWN2: ("down2", down.at[:, 2]),
    }

    @pl.when(layer > 0)
    def _():
        loads["cpl"].wait()
        turned = jnp.stack([cpl[0].T, cpl[1].T])[None]
        real, imag = times(turned, wh[INV], wl[INV])
        gt[0, 0] = -real[0]
        gt[0, 1] = -imag[0]
        gt_copy.start()

        @pl.loop(0, chunks)
        def _(at):
            couple(at)

        gt_copy.wait()
        real, imag = times(gt_in[...], wh[UP0], wl[UP0])
        for row, pair in ((0, (gt[0, 0], gt[0, 1])), (border, (real[0], imag[0]))):
            for part in range(2):
                high, low = split(pair[part])
                ah[row : row + border, part * size : (part + 1) * size] = high
                al[row : row + border, part * size : (part + 1) * size] = low

        for at, (name, matrix) in sources_of.items():
            if at != TURN:
                if at != UP1:
                    loads[name].wait()
                prepare(at, matrix)
        prepare_border()
        up1_copy.wait()
        down2_copy.start()
        product(UP21, UP2, far.at[0])
        up4_copy.wait()
        product(TURN, TURN2, far.at[1])
        prepare(TURN2, up.at[:, 4], down.at[:, 4])

        @pl.when(layer > 1)
        def _():
            down2_copy.wait()
            product(DOWN12, DOWN1, far.at[2])

    @pl.when(layer == 0)
    def _():
        loads["cpl"].wait()

    def b_copy(block, side):
        target = partners[1] if side else leaf
        return pltpu.make_async_remote_copy(
            sb.at[block], rb.at[block, side], b_send.at[side], b_recv.at[block, side],
            device_id=(below, target), device_id_type=MESH,
        )

    def sweep(moves, order, plain):
        lags = dict(order)
        final = len(moves)

        def front(stage, block):
            return s_last.at[block] if stage == final - 1 else s.at[stage, block]

        def arrived(lane, block):
            return r_last.at[block] if lane == LAST else r.at[lane, block % SLOTS]

        def f_copy(stage, lane, mask, block):
            return pltpu.make_async_remote_copy(
                front(stage, block), arrived(lane, block), send.at[lane], recv.at[lane, block % SLOTS],
                device_id=(layer, partners[mask]), device_id_type=MESH,
            )

        senders = {lane: (stage, mask) for stage, move in enumerate(moves) for lane, mask in move[3]}

        def receive(lane, block):
            stage, mask = senders[lane]
            f_copy(stage, lane, mask, block).wait_recv()

        def stage_first(block):
            if plain:

                @pl.when(block % CHUNK == 0)
                def _():
                    couple(block // CHUNK)

                front(0, block)[...] = g[block]
            else:
                for side in range(2):
                    b_copy(block, side).wait_recv()
                v = jnp.concatenate([rb[block, 0], rb[block, 1]], axis=-1)[None]
                real, imag = times(v, ah[...], al[...])
                front(0, block)[0] = g[block, 0] + real[0]
                front(0, block)[1] = g[block, 1] + imag[0]

        def stage_middle(stage, block):
            lanes, at, own, _ = moves[stage]
            if plain:

                @pl.when(block == 0)
                def _():
                    name, matrix = sources_of[at]
                    loads[name].wait()
                    prepare(at, matrix)

            if stage >= LATE and not plain:

                @pl.when(jnp.logical_and(block == 0, layer == 1))
                def _():
                    if stage == LATE:
                        down2_copy.wait()
                    product(DOWN12, DOWN1, far.at[2], (stage - LATE,))

            for lane in lanes:
                receive(lane, block)
            past = front(stage - 1, block)[...]
            terms = [past] if own else []
            terms += [arrived(lane, block)[...] for lane in lanes]
            total = past[0], past[1]
            for index, term in enumerate(terms):
                real, imag = times(term[None], wh[at + index], wl[at + index])
                total = total[0] + real[0], total[1] + imag[0]
            front(stage, block)[0] = total[0]
            front(stage, block)[1] = total[1]

        def stage_border(block):
            if plain:

                @pl.when(block == 0)
                def _():
                    prepare_border()

            @pl.when(layer < layers - 1)
            def _():
                high, low = split(front(final - 1, block)[...].reshape(2 * WIDTH, size))
                own = jnp.dot(jnp.concatenate([high, low], axis=0), take[...], preferred_element_type=F32)
                own = (own[: 2 * WIDTH] + own[2 * WIDTH :]).reshape(2, WIDTH, border)
                receive(LAST, block)
                real, imag = times(arrived(LAST, block)[...][None], eh[...], el[...])
                sb[block, 0] = own[0] + real[0]
                sb[block, 1] = own[1] + imag[0]
                for side in range(2):
                    b_copy(block, side).start()

            @pl.when(layer == layers - 1)
            def _():
                receive(LAST, block)

        count = 128 // WIDTH

        def stage_output(half):
            part = pl.ds(half * count, count)
            real, imag = times(r_last[part], wh[DOWN0], wl[DOWN0])
            for index, add in ((0, real), (1, imag)):
                x = (s_last[part, index] + add).reshape(128, size)
                y = None
                for term in split(x):
                    value = jnp.dot(term, pick[...], preferred_element_type=F32)
                    y = value if y is None else y + value
                out_ref[index, :, half * 128 : (half + 1) * 128] = y.T

        @pl.loop(0, blocks + max(lags.values()))
        def _(tick):
            for stage, lag in order:
                block = tick - lag

                @pl.when(jnp.logical_and(block >= 0, block < blocks))
                def _():
                    if stage == final:
                        stage_border(block)
                        return
                    if stage == 0:
                        stage_first(block)
                    else:
                        stage_middle(stage, block)
                    for lane, mask in moves[stage][3]:
                        f_copy(stage, lane, mask, block).start()

            for half in range(columns // 128):

                @pl.when(tick == lags[final] + (half + 1) * count - 1)
                def _():
                    stage_output(half)

        for lane, (stage, mask) in senders.items():
            every = s_last if lane == LAST else s.at[stage]
            pltpu.make_async_remote_copy(
                every, every, send.at[lane], recv.at[0, 0], device_id=(layer, partners[mask]), device_id_type=MESH
            ).wait_send()

    @pl.when(layer == 0)
    def _():
        sweep(PLAIN, PLAIN_ORDER, True)

    @pl.when(layer > 0)
    def _():
        sweep(FUSED, FUSED_ORDER, False)

    @pl.when(layer < layers - 1)
    def _():
        for side in range(2):
            pltpu.make_async_remote_copy(
                sb, sb, b_send.at[side], b_recv.at[0, 0], device_id=(below, leaf), device_id_type=MESH
            ).wait_send()


def per_device(sources, leaf_inverse, tree_up, tree_down, coupling, index_map):
    size, columns = sources.shape[-2:]
    border = coupling.shape[-1]
    levels = tree_up.shape[3]
    blocks = columns // WIDTH
    operands = (
        sources.reshape(2, size, columns),
        leaf_inverse.reshape(2, size, size),
        tree_up.reshape(2, levels, size, size),
        tree_down.reshape(2, levels, size, size),
        coupling.reshape(2, size, border),
        index_map.reshape(1, size),
    )
    vmem, dma = pltpu.VMEM, pltpu.SemaphoreType.DMA
    wide = 2 * size
    out = pl.pallas_call(
        kernel,
        out_shape=jax.ShapeDtypeStruct((2, size, columns), F32),
        in_specs=[pl.BlockSpec(memory_space=pl.ANY)] * 5 + [pl.BlockSpec(memory_space=pltpu.VMEM)],
        out_specs=pl.BlockSpec(memory_space=pltpu.VMEM),
        scratch_shapes=[
            vmem((2, size, columns), F32),
            vmem((2, size, size), F32),
            vmem((2, levels, size, size), F32),
            vmem((2, levels, size, size), F32),
            vmem((2, size, border), F32),
            vmem((13, size, wide), BF16),
            vmem((13, size, wide), BF16),
            vmem((2 * border, wide), BF16),
            vmem((2 * border, wide), BF16),
            vmem((size, 2 * border), BF16),
            vmem((size, 2 * border), BF16),
            vmem((size, size), BF16),
            vmem((size, size), BF16),
            vmem((size, border), BF16),
            vmem((3, 2, size, size), F32),
            vmem((blocks, 2, WIDTH, size), F32),
            vmem((blocks, 2, WIDTH, size), F32),
            vmem((1, 2, border, size), F32),
            vmem((1, 2, border, size), F32),
            vmem((len(PLAIN) - 1, blocks, 2, WIDTH, size), F32),
            vmem((LAST, SLOTS, 2, WIDTH, size), F32),
            vmem((blocks, 2, WIDTH, size), F32),
            vmem((blocks, 2, WIDTH, size), F32),
            vmem((blocks, 2, WIDTH, border), F32),
            vmem((blocks, 2, 2, WIDTH, border), F32),
            dma((4 + 2 * levels,)),
            dma((blocks // CHUNK,)),
            dma((blocks // CHUNK,)),
            dma,
            dma,
            dma((3,)),
            dma((3,)),
            dma((LAST + 1,)),
            dma((LAST + 1, SLOTS)),
            dma((2,)),
            dma((blocks, 2)),
        ],
        compiler_params=pltpu.CompilerParams(
            collective_id=0, has_side_effects=True, vmem_limit_bytes=60 * 1024 * 1024
        ),
        name="sweep",
    )(*operands)
    return out.reshape(sources.shape)


def solution(mesh):
    placed = (
        P(None, "layer", "leaf", None, None),
        P(None, "layer", "leaf", None, None),
        P(None, "layer", "leaf", None, None, None),
        P(None, "layer", "leaf", None, None, None),
        P(None, "layer", "leaf", None, None),
        P("layer", "leaf", None),
    )
    return jax.shard_map(
        per_device,
        mesh=mesh,
        in_specs=placed,
        out_specs=P(None, "layer", "leaf", None, None),
        check_vma=False,
    )
```

```python
import jax
import jax.numpy as jnp
from jax import lax
from jax.experimental import pallas as pl
from jax.experimental.pallas import tpu as pltpu
from jax.sharding import PartitionSpec as P

MESH = pl.DeviceIdType.MESH
F32, BF16 = jnp.float32, jnp.bfloat16
WIDTH = 16
SLOTS = 4
CHUNK = 4

UP1, UP2, UP21, UP3, TURN, TURN2, DOWN3, DOWN1, DOWN2, DOWN12, UP0, INV, DOWN0 = range(13)
LAST = 9

PLAIN = (
    ((), None, False, ((0, 2),)),
    ((0,), UP1, False, ((1, 4),)),
    ((1,), UP2, False, ((3, 8),)),
    ((3,), UP3, False, ((4, 16),)),
    ((4,), TURN, False, ((2, 16),)),
    ((2,), TURN2, False, ((5, 8),)),
    ((5,), DOWN3, False, ((7, 4),)),
    ((7,), DOWN2, False, ((6, 2),)),
    ((6,), DOWN1, False, ((LAST, 1),)),
)
FUSED = (
    ((), None, False, ((1, 4), (0, 2), (2, 6))),
    ((0, 1, 2), UP1, False, ((3, 8),)),
    ((3,), UP3, False, ((4, 16),)),
    ((4,), TURN, True, ((5, 8),)),
    ((5,), DOWN3, False, ((7, 4), (6, 2), (8, 6))),
    ((6, 7, 8), DOWN1, False, ((LAST, 1),)),
)
MASKS = (1, 2, 4, 6, 8, 16)
LATE = 3

PLAIN_ORDER = ((0, 0), (9, 12), (5, 8), (6, 9), (8, 11), (7, 10), (2, 3), (4, 6), (1, 1), (3, 4))
FUSED_ORDER = ((0, 0), (2, 3), (3, 4), (4, 5), (6, 7), (1, 1), (5, 6))


def split(x):
    high = x.astype(BF16)
    return high, (x - high.astype(F32)).astype(BF16)


def times(v, high, low):
    blocks, _, width, depth = v.shape
    rows, n = blocks * 2 * width, high.shape[1] // 2
    v_high, v_low = split(v.reshape(rows, depth))
    p = jnp.dot(jnp.concatenate([v_high, v_low], axis=0), high, preferred_element_type=F32)
    r = p[:rows] + p[rows:] + jnp.dot(v_high, low, preferred_element_type=F32)
    r = r.reshape(blocks, 2, width, 2 * n)
    return r[:, 0, :, :n] - r[:, 1, :, n:], r[:, 0, :, n:] + r[:, 1, :, :n]


def kernel(
    src_hbm, inv_hbm, up_hbm, down_hbm, cpl_hbm, row_ref, out_ref,
    src, inv, up, down, cpl, wh, wl, ah, al, eh, el, place, pick, take, far,
    g, g_in, gt, gt_in, s, r, s_last, r_last, sb, rb,
    in_sem, g_send, g_recv, gt_send, gt_recv, far_send, far_recv, send, recv, b_send, b_recv,
):
    size = inv.shape[-1]
    border = cpl.shape[-1]
    columns = src.shape[-1]
    blocks = columns // WIDTH
    levels = up.shape[1]
    layers = lax.axis_size("layer")
    layer, leaf = lax.axis_index("layer"), lax.axis_index("leaf")

    def mirror(mask):
        other = leaf
        for bit in range(levels):
            if mask >> bit & 1:
                other = other + (1 - 2 * ((leaf // (1 << bit)) % 2)) * (1 << bit)
        return other

    below, above = (layer + 1) % layers, (layer + layers - 1) % layers
    partners = {mask: mirror(mask) for mask in MASKS}

    loads = {}

    def load(name, source, target):
        loads[name] = pltpu.make_async_copy(source, target, in_sem.at[len(loads)])
        loads[name].start()

    load("inv", inv_hbm, inv)
    load("src", src_hbm, src)
    load("up0", up_hbm.at[:, 0], up.at[:, 0])

    barrier = pltpu.get_barrier_semaphore()
    neighbours = [(layer, p) for p in partners.values()]
    neighbours += [(z, q) for z in (below, above) for q in (leaf, partners[1])]
    for device in neighbours:
        pl.semaphore_signal(barrier, inc=1, device_id=device, device_id_type=MESH)

    sublane = lax.broadcasted_iota(jnp.int32, (size, size), 0)
    chosen = jnp.where(sublane == row_ref[...], 1.0, 0.0)
    place[...] = chosen.astype(BF16)
    pick[...] = chosen.T.astype(BF16)

    def prepare(at, *matrices):
        for part in range(2):
            total = matrices[0][part]
            for matrix in matrices[1:]:
                total = total + matrix[part]
            high, low = split(total.T)
            wh[at, :, part * size : (part + 1) * size] = high
            wl[at, :, part * size : (part + 1) * size] = low

    loads["inv"].wait()
    prepare(INV, inv)
    for w in (wh, wl):
        w[INV] = jnp.dot(place[...], w[INV], preferred_element_type=F32).astype(BF16)

    loads["src"].wait()
    for bit in (1, 4):
        load(f"up{bit}", up_hbm.at[:, bit], up.at[:, bit])
    load("cpl", cpl_hbm, cpl)
    load("down2", down_hbm.at[:, 2], down.at[:, 2])
    for bit in (2, 3):
        load(f"up{bit}", up_hbm.at[:, bit], up.at[:, bit])
    for bit in (4, 3, 1, 0):
        load(f"down{bit}", down_hbm.at[:, bit], down.at[:, bit])

    for half in range(columns // 128):
        count = 128 // WIDTH
        for part in range(2):
            turned = src[part, :, half * 128 : (half + 1) * 128].T
            g[half * count : (half + 1) * count, part] = turned.reshape(count, WIDTH, size)
    pl.semaphore_wait(barrier, len(neighbours))

    chunks = blocks // CHUNK

    def g_copy(at):
        part = pl.ds(at * CHUNK, CHUNK)
        return pltpu.make_async_remote_copy(
            g.at[part], g_in.at[part], g_send.at[at], g_recv.at[at],
            device_id=(layer, partners[1]), device_id_type=MESH,
        )

    def far_copy(at, source, mask):
        return pltpu.make_async_remote_copy(
            source, far.at[at], far_send.at[at], far_recv.at[at],
            device_id=(layer, partners[mask]), device_id_type=MESH,
        )

    up1_copy = far_copy(0, up.at[:, 1], 4)
    up4_copy = far_copy(1, up.at[:, 4], 16)
    down2_copy = far_copy(2, down.at[:, 2], 2)

    @pl.when(layer > 0)
    def _():
        loads["up1"].wait()
        up1_copy.start()
        loads["up4"].wait()
        up4_copy.start()

    def lead(at):
        part = pl.ds(at * CHUNK, CHUNK)
        real, imag = times(g[part], wh[INV], wl[INV])
        g[part, 0] = real
        g[part, 1] = imag
        g_copy(at).start()

    @pl.loop(0, jnp.where(layer == 0, 1, chunks))
    def _(at):
        lead(at)

    loads["up0"].wait()
    prepare(UP0, up.at[:, 0])

    def couple(at):
        part = pl.ds(at * CHUNK, CHUNK)
        g_copy(at).wait()
        real, imag = times(g_in[part], wh[UP0], wl[UP0])
        g[part, 0] = g[part, 0] + real
        g[part, 1] = g[part, 1] + imag

    def product(at, by, matrix, parts=(0, 1, 2)):
        for low_row in (part * (size // 3) for part in parts):
            rows = slice(low_row, low_row + 128)
            v = jnp.stack([matrix[0, :, rows].T, matrix[1, :, rows].T])[None]
            for part, value in enumerate(times(v, wh[by], wl[by])):
                high, low = split(value[0])
                wh[at, rows, part * size : (part + 1) * size] = high
                wl[at, rows, part * size : (part + 1) * size] = low

    def prepare_border():
        loads["down0"].wait()
        prepare(DOWN0, down.at[:, 0])
        take[...] = pick[:, size - border :]
        for w, e in ((wh, eh), (wl, el)):
            for part in range(2):
                e[:, part * border : (part + 1) * border] = jnp.dot(
                    w[DOWN0, :, part * size : (part + 1) * size], take[...], preferred_element_type=F32
                ).astype(BF16)

    gt_copy = pltpu.make_async_remote_copy(
        gt, gt_in, gt_send, gt_recv, device_id=(layer, partners[1]), device_id_type=MESH
    )
    sources_of = {
        UP1: ("up1", up.at[:, 1]), UP2: ("up2", up.at[:, 2]), UP3: ("up3", up.at[:, 3]), TURN: ("up4", up.at[:, 4]),
        TURN2: ("down4", down.at[:, 4]), DOWN3: ("down3", down.at[:, 3]), DOWN1: ("down1", down.at[:, 1]),
        DOWN2: ("down2", down.at[:, 2]),
    }

    @pl.when(layer > 0)
    def _():
        loads["cpl"].wait()
        turned = jnp.stack([cpl[0].T, cpl[1].T])[None]
        real, imag = times(turned, wh[INV], wl[INV])
        gt[0, 0] = -real[0]
        gt[0, 1] = -imag[0]
        gt_copy.start()

        @pl.loop(0, chunks)
        def _(at):
            couple(at)

        gt_copy.wait()
        real, imag = times(gt_in[...], wh[UP0], wl[UP0])
        for row, pair in ((0, (gt[0, 0], gt[0, 1])), (border, (real[0], imag[0]))):
            for part in range(2):
                high, low = split(pair[part])
                ah[row : row + border, part * size : (part + 1) * size] = high
                al[row : row + border, part * size : (part + 1) * size] = low

        for at, (name, matrix) in sources_of.items():
            if at != TURN:
                if at != UP1:
                    loads[name].wait()
                prepare(at, matrix)
        prepare_border()
        up1_copy.wait()
        down2_copy.start()
        product(UP21, UP2, far.at[0])
        up4_copy.wait()
        product(TURN, TURN2, far.at[1])
        prepare(TURN2, up.at[:, 4], down.at[:, 4])

        @pl.when(layer > 1)
        def _():
            down2_copy.wait()
            product(DOWN12, DOWN1, far.at[2])

    @pl.when(layer == 0)
    def _():
        loads["cpl"].wait()

    def b_copy(block, side):
        target = partners[1] if side else leaf
        return pltpu.make_async_remote_copy(
            sb.at[block], rb.at[block, side], b_send.at[side], b_recv.at[block, side],
            device_id=(below, target), device_id_type=MESH,
        )

    def sweep(moves, order, plain):
        lags = dict(order)
        final = len(moves)

        def front(stage, block):
            return s_last.at[block] if stage == final - 1 else s.at[stage, block]

        def arrived(lane, block):
            return r_last.at[block] if lane == LAST else r.at[lane, block % SLOTS]

        def f_copy(stage, lane, mask, block):
            return pltpu.make_async_remote_copy(
                front(stage, block), arrived(lane, block), send.at[lane], recv.at[lane, block % SLOTS],
                device_id=(layer, partners[mask]), device_id_type=MESH,
            )

        senders = {lane: (stage, mask) for stage, move in enumerate(moves) for lane, mask in move[3]}

        def receive(lane, block):
            stage, mask = senders[lane]
            f_copy(stage, lane, mask, block).wait_recv()

        def stage_first(block):
            if plain:

                @pl.when(block % CHUNK == 0)
                def _():
                    couple(block // CHUNK)

                @pl.when(jnp.logical_and(block % CHUNK == 1, block < blocks - CHUNK))
                def _():
                    lead(block // CHUNK + 1)

                front(0, block)[...] = g[block]
            else:
                for side in range(2):
                    b_copy(block, side).wait_recv()
                v = jnp.concatenate([rb[block, 0], rb[block, 1]], axis=-1)[None]
                real, imag = times(v, ah[...], al[...])
                front(0, block)[0] = g[block, 0] + real[0]
                front(0, block)[1] = g[block, 1] + imag[0]

        def stage_middle(stage, block):
            lanes, at, own, _ = moves[stage]
            if plain:

                @pl.when(block == 0)
                def _():
                    name, matrix = sources_of[at]
                    loads[name].wait()
                    prepare(at, matrix)

            if stage >= LATE and not plain:

                @pl.when(jnp.logical_and(block == 0, layer == 1))
                def _():
                    if stage == LATE:
                        down2_copy.wait()
                    product(DOWN12, DOWN1, far.at[2], (stage - LATE,))

            for lane in lanes:
                receive(lane, block)
            past = front(stage - 1, block)[...]
            terms = [past] if own else []
            terms += [arrived(lane, block)[...] for lane in lanes]
            total = past[0], past[1]
            for index, term in enumerate(terms):
                real, imag = times(term[None], wh[at + index], wl[at + index])
                total = total[0] + real[0], total[1] + imag[0]
            front(stage, block)[0] = total[0]
            front(stage, block)[1] = total[1]

        def stage_border(block):
            if plain:

                @pl.when(block == 0)
                def _():
                    prepare_border()

            @pl.when(layer < layers - 1)
            def _():
                high, low = split(front(final - 1, block)[...].reshape(2 * WIDTH, size))
                own = jnp.dot(jnp.concatenate([high, low], axis=0), take[...], preferred_element_type=F32)
                own = (own[: 2 * WIDTH] + own[2 * WIDTH :]).reshape(2, WIDTH, border)
                receive(LAST, block)
                real, imag = times(arrived(LAST, block)[...][None], eh[...], el[...])
                sb[block, 0] = own[0] + real[0]
                sb[block, 1] = own[1] + imag[0]
                for side in range(2):
                    b_copy(block, side).start()

            @pl.when(layer == layers - 1)
            def _():
                receive(LAST, block)

        count = 128 // WIDTH

        def stage_output(half):
            part = pl.ds(half * count, count)
            real, imag = times(r_last[part], wh[DOWN0], wl[DOWN0])
            for index, add in ((0, real), (1, imag)):
                x = (s_last[part, index] + add).reshape(128, size)
                y = None
                for term in split(x):
                    value = jnp.dot(term, pick[...], preferred_element_type=F32)
                    y = value if y is None else y + value
                out_ref[index, :, half * 128 : (half + 1) * 128] = y.T

        @pl.loop(0, blocks + max(lags.values()))
        def _(tick):
            for stage, lag in order:
                block = tick - lag

                @pl.when(jnp.logical_and(block >= 0, block < blocks))
                def _():
                    if stage == final:
                        stage_border(block)
                        return
                    if stage == 0:
                        stage_first(block)
                    else:
                        stage_middle(stage, block)
                    for lane, mask in moves[stage][3]:
                        f_copy(stage, lane, mask, block).start()

            for half in range(columns // 128):

                @pl.when(tick == lags[final] + (half + 1) * count - 1)
                def _():
                    stage_output(half)

        for lane, (stage, mask) in senders.items():
            every = s_last if lane == LAST else s.at[stage]
            pltpu.make_async_remote_copy(
                every, every, send.at[lane], recv.at[0, 0], device_id=(layer, partners[mask]), device_id_type=MESH
            ).wait_send()

    @pl.when(layer == 0)
    def _():
        sweep(PLAIN, PLAIN_ORDER, True)

    @pl.when(layer > 0)
    def _():
        sweep(FUSED, FUSED_ORDER, False)

    @pl.when(layer < layers - 1)
    def _():
        for side in range(2):
            pltpu.make_async_remote_copy(
                sb, sb, b_send.at[side], b_recv.at[0, 0], device_id=(below, leaf), device_id_type=MESH
            ).wait_send()


def per_device(sources, leaf_inverse, tree_up, tree_down, coupling, index_map):
    size, columns = sources.shape[-2:]
    border = coupling.shape[-1]
    levels = tree_up.shape[3]
    blocks = columns // WIDTH
    operands = (
        sources.reshape(2, size, columns),
        leaf_inverse.reshape(2, size, size),
        tree_up.reshape(2, levels, size, size),
        tree_down.reshape(2, levels, size, size),
        coupling.reshape(2, size, border),
        index_map.reshape(1, size),
    )
    vmem, dma = pltpu.VMEM, pltpu.SemaphoreType.DMA
    wide = 2 * size
    out = pl.pallas_call(
        kernel,
        out_shape=jax.ShapeDtypeStruct((2, size, columns), F32),
        in_specs=[pl.BlockSpec(memory_space=pl.ANY)] * 5 + [pl.BlockSpec(memory_space=pltpu.VMEM)],
        out_specs=pl.BlockSpec(memory_space=pltpu.VMEM),
        scratch_shapes=[
            vmem((2, size, columns), F32),
            vmem((2, size, size), F32),
            vmem((2, levels, size, size), F32),
            vmem((2, levels, size, size), F32),
            vmem((2, size, border), F32),
            vmem((13, size, wide), BF16),
            vmem((13, size, wide), BF16),
            vmem((2 * border, wide), BF16),
            vmem((2 * border, wide), BF16),
            vmem((size, 2 * border), BF16),
            vmem((size, 2 * border), BF16),
            vmem((size, size), BF16),
            vmem((size, size), BF16),
            vmem((size, border), BF16),
            vmem((3, 2, size, size), F32),
            vmem((blocks, 2, WIDTH, size), F32),
            vmem((blocks, 2, WIDTH, size), F32),
            vmem((1, 2, border, size), F32),
            vmem((1, 2, border, size), F32),
            vmem((len(PLAIN) - 1, blocks, 2, WIDTH, size), F32),
            vmem((LAST, SLOTS, 2, WIDTH, size), F32),
            vmem((blocks, 2, WIDTH, size), F32),
            vmem((blocks, 2, WIDTH, size), F32),
            vmem((blocks, 2, WIDTH, border), F32),
            vmem((blocks, 2, 2, WIDTH, border), F32),
            dma((4 + 2 * levels,)),
            dma((blocks // CHUNK,)),
            dma((blocks // CHUNK,)),
            dma,
            dma,
            dma((3,)),
            dma((3,)),
            dma((LAST + 1,)),
            dma((LAST + 1, SLOTS)),
            dma((2,)),
            dma((blocks, 2)),
        ],
        compiler_params=pltpu.CompilerParams(
            collective_id=0, has_side_effects=True, vmem_limit_bytes=60 * 1024 * 1024
        ),
        name="sweep",
    )(*operands)
    return out.reshape(sources.shape)


def solution(mesh):
    placed = (
        P(None, "layer", "leaf", None, None),
        P(None, "layer", "leaf", None, None),
        P(None, "layer", "leaf", None, None, None),
        P(None, "layer", "leaf", None, None, None),
        P(None, "layer", "leaf", None, None),
        P("layer", "leaf", None),
    )
    return jax.shard_map(
        per_device,
        mesh=mesh,
        in_specs=placed,
        out_specs=P(None, "layer", "leaf", None, None),
        check_vma=False,
    )
```
